32 devices in a mesh: cells: 8 (over z, x), snap: 4 (over y, core).
Axes of the slice: x: 2, y: 2, z: 4, core: 2. Of those that a mesh axis runs over, the one named last changes fastest.
Arguments:
- temporal_modes: bfloat16 [256, 4096], P('cells', 'snap'), may hold values from -0.09375 to 0.09375
- volume_field: bfloat16 [4096, 20480], P('snap', 'cells'), may hold values from -6 to 6
- mass_root: float32 [20480], P('cells'), may hold values from 0.3 to 3
- wall_pressure: bfloat16 [5120, 4096], P('cells', 'snap'), may hold values from -6 to 6
- face_area: bfloat16 [5120], P('cells'), may hold values from 0.099609375 to 10
- face_count: int32 [8], P('cells'), may hold values from 0 to 640, as said below
Outputs:
- extended_modes: bfloat16 [256, 20480], P('snap', 'cells')
- wall_modes: bfloat16 [5120, 256], P('cells')
The draws below stay inside these ranges and needn't reach their ends.
Inputs may be any that keep to these rules, and one draw needn't show every extreme that they name: `face_count`: exactly 2 partitions have live wall faces, each between 320 and 640 of them, and one has exactly 640; every other partition has none.
All inputs are finite; a program needn't handle non-finite values.
Results may differ from the reference program's by a relative error of at most 0.013.
Values may be sent and summed in bfloat16 or wider, within the bound.
A program may use at most 64 MiB of HBM per device.

```python
import math
import jax
import jax.numpy as jnp
from jax import lax

MODES = 256
SNAP_DEV = 1024
FACE_DEV = 640
SNAPS = 4096
CELLS = 20480
WALL_SLOTS = 5120
OWNERS = 2
N_CELLS = 8
N_SNAP = 4


def draw_face_count(key, part):
    order_key, count_key = jax.random.split(jax.random.fold_in(key, 17))
    ranking = jax.random.permutation(order_key, N_CELLS).astype(jnp.int32)
    drawn = jax.random.randint(count_key, (N_CELLS,), FACE_DEV // 2, FACE_DEV + 1).astype(jnp.int32)
    counts = jnp.where(ranking == 0, FACE_DEV, drawn)
    return jnp.where(ranking < OWNERS, counts, 0).astype(jnp.int32)


def block_levels(own_key, dims, pieces, smallest, high):
    def one(position, shards_of):
        heights = jax.random.uniform(jax.random.fold_in(jax.random.fold_in(own_key, 6), position), (shards_of,), jnp.float32, smallest / len(pieces), high / len(pieces))
        return jnp.repeat(jnp.exp(heights), dims[position] // shards_of).reshape((-1,) + (1,) * (len(dims) - position - 1))

    factor_of = one(*pieces[0])
    for cut in pieces[1:]:
        factor_of = factor_of * one(*cut)
    return factor_of


def normal_values(rng, dims, scale, reach, cuts=(), held_as=jnp.bfloat16):
    entries = scale * jax.random.normal(rng, dims, jnp.float32)
    if cuts:
        entries = entries * block_levels(rng, dims, cuts, -0.22, 0.18)
    return jnp.clip(entries, -reach, reach).astype(held_as)


def setup_inputs(seed: int = 0) -> dict:
    streams_of = jax.random.split(jax.random.key(seed), 7)
    temporal_modes = normal_values(streams_of[0], (MODES, SNAPS), SNAPS ** -0.5, 0.09375, ((0, 8), (1, 4)))
    volume_field = normal_values(streams_of[1], (SNAPS, CELLS), 1.0, 6.0, ((0, 4), (1, 8)))
    mass_root = jnp.clip(jnp.exp(math.log(3.0) - 2.3025851 * jax.random.uniform(streams_of[2], (CELLS,), jnp.float32) ** block_levels(streams_of[2], (CELLS,), ((0, 8),), -0.2, 0.2)), 0.3, 3.0)
    wall_pressure = normal_values(streams_of[3], (WALL_SLOTS, SNAPS), 1.0, 6.0, ((0, 8), (1, 4)))
    face_area = jnp.clip(jnp.exp(math.log(10.0) - 4.609084 * jax.random.uniform(streams_of[4], (WALL_SLOTS,), jnp.float32) ** block_levels(streams_of[4], (WALL_SLOTS,), ((0, 8),), -0.2, 0.2)), 0.099609375, 10.0).astype(jnp.bfloat16)
    face_count = draw_face_count(jax.random.fold_in(streams_of[6], 71), 0)
    return {"temporal_modes": temporal_modes, "volume_field": volume_field, "mass_root": mass_root, "wall_pressure": wall_pressure, "face_area": face_area, "face_count": face_count}


def reference(temporal_modes, volume_field, mass_root, wall_pressure, face_area, face_count):
    slot = jnp.arange(WALL_SLOTS, dtype=jnp.int32)
    owner = (slot // FACE_DEV).astype(jnp.int32)
    live = slot % FACE_DEV < face_count[owner]
    live_area = jnp.where(live, face_area.astype(jnp.float32), jnp.float32(0.0))
    wall_coef = lax.dot_general(wall_pressure, temporal_modes, (((1,), (1,)), ((), ())), preferred_element_type=jnp.float32)
    energy = lax.optimization_barrier(jnp.sum(live_area[:, None] * wall_coef * wall_coef, axis=0)) / jnp.sum(live_area)
    inverse = lax.rsqrt(energy + 1e-06)
    wall_modes = jnp.where(live[:, None], wall_coef * inverse[None, :], jnp.float32(0.0)).astype(jnp.bfloat16)
    projection = jnp.zeros((MODES, CELLS), jnp.float32)
    for block in range(N_SNAP):
        lower = block * SNAP_DEV
        partial_b = jnp.dot(temporal_modes[:, lower:lower + SNAP_DEV], volume_field[lower:lower + SNAP_DEV], preferred_element_type=jnp.float32)
        rounded = lax.optimization_barrier(partial_b.astype(jnp.bfloat16))
        projection = projection + rounded.astype(jnp.float32)
    scaled = projection * mass_root[None, :] * inverse[:, None]
    return (scaled.astype(jnp.bfloat16), wall_modes)
```

```python
import functools

import jax
import jax.numpy as jnp
from jax import lax
from jax.experimental import pallas as pl
from jax.experimental.pallas import tpu as pltpu
from jax.sharding import PartitionSpec as P

MESH = pl.DeviceIdType.MESH
F32 = jnp.float32
BF16 = jnp.bfloat16
LANES = 128


def kernel(
    n, lines, pieces,
    modes_ref, vol_ref, mass_ref, press_ref, area_ref, count_ref,
    ext_ref, wall_ref,
    gbuf, perm, vbuf, pbuf, wcol,
    w_send, w_recv, w_keep, wy_send, wy_recv, coef,
    p_send, p_recv, p_keep, py_send, py_recv,
    e_send, e_recv, inv_row, inv_col, ext_buf, wall_buf,
    load_sem, g_send_sem, g_recv_sem, w_sem, p_sem, py_sem, e_send_sem, e_recv_sem, out_sem,
):
    cell, snap = lax.axis_index("cells"), lax.axis_index("snap")
    y, core = snap // 2, snap % 2
    group = n // lines
    z, x = cell // group, cell % group
    mate = (cell, y * 2 + 1 - core)
    across = (cell, (1 - y) * 2 + core)
    others = [(lax.rem(cell + d, n), snap) for d in range(1, n)]
    mode_count, depth = perm.shape
    share = mode_count // 4
    per_share = n // 4
    half = pbuf.shape[1]
    width = vbuf.shape[2]
    slots = 2 * half

    def remote(src, dst, send, recv, to):
        return pltpu.make_async_remote_copy(
            src_ref=src, dst_ref=dst, send_sem=send, recv_sem=recv,
            device_id=to, device_id_type=MESH,
        )

    own_copy = pltpu.make_async_copy(modes_ref, gbuf.at[cell], load_sem.at[0])
    own_copy.start()
    press_copies = [
        pltpu.make_async_copy(press_ref.at[pl.ds(h * half, half)], pbuf.at[h], load_sem.at[1 + h])
        for h in range(2)
    ]
    vol_copies = [
        pltpu.make_async_copy(vol_ref.at[:, pl.ds(j * width, width)], vbuf.at[j], load_sem.at[3 + j])
        for j in range(pieces)
    ]
    for copy in press_copies + vol_copies:
        copy.start()

    barrier = pltpu.get_barrier_semaphore()
    greeted = others + [mate, across]
    for other in greeted:
        pl.semaphore_signal(barrier, inc=1, device_id=other, device_id_type=MESH)
    pl.semaphore_wait(barrier, len(greeted))

    sent = []
    beside = [z * group + lax.rem(x + d, group) for d in range(1, group)]
    for d, to in enumerate(beside):
        copy = remote(modes_ref, gbuf.at[cell], g_send_sem.at[0, d], g_recv_sem.at[cell], (to, snap))
        copy.start()
        sent.append(copy)
    along = [lax.rem(z + d, lines) * group + x for d in range(1, lines)]
    for d, to in enumerate(along):
        copy = remote(
            modes_ref, gbuf.at[cell], g_send_sem.at[0, group - 1 + d], g_recv_sem.at[cell], (to, snap)
        )
        copy.start()
        sent.append(copy)

    slot_row = lax.broadcasted_iota(jnp.int32, (1, LANES), 1)
    count = count_ref[0]
    area_lanes = jnp.zeros((1, LANES), F32)
    for i in range(slots // LANES):
        row = area_ref[i : i + 1, :].astype(F32)
        row = jnp.where(slot_row + i * LANES < count, row, 0.0)
        area_lanes = area_lanes + row
        wcol[pl.ds(i * LANES, LANES), :] = jnp.broadcast_to(row, (LANES, LANES)).T

    for d, origin in enumerate(along):
        remote(
            gbuf.at[origin], gbuf.at[origin], g_send_sem.at[0, 0], g_recv_sem.at[origin], (origin, snap)
        ).wait_recv()
        for i, to in enumerate(beside):
            copy = remote(
                gbuf.at[origin], gbuf.at[origin], g_send_sem.at[1 + d, i], g_recv_sem.at[origin], (to, snap)
            )
            copy.start()
            sent.append(copy)
    own_copy.wait()
    for side in beside:
        for d in range(lines):
            origin = lax.rem(z + d, lines) * group + lax.rem(side, group)
            remote(
                gbuf.at[origin], gbuf.at[origin], g_send_sem.at[0, 0], g_recv_sem.at[origin], (side, snap)
            ).wait_recv()

    all_modes = gbuf[...].reshape(mode_count, depth).astype(BF16)
    for copy in press_copies:
        copy.wait()

    def contract(h):
        return lax.dot_general(
            pbuf[h], all_modes, (((1,), (1,)), ((), ())), preferred_element_type=F32
        )

    w_send[...] = contract(1 - core).astype(BF16)
    w_mate = remote(w_send, w_recv, w_sem.at[0], w_sem.at[1], mate)
    w_mate.start()
    w_keep[...] = contract(core)

    order = [
        (1 - y) * 2 + 1 - core, y * 2 + 1 - core, (1 - y) * 2 + core, y * 2 + core,
    ]
    for i, s in enumerate(order):
        perm[pl.ds(i * share, share), :] = (
            gbuf[pl.ds(s * per_share, per_share)].reshape(share, depth).astype(BF16)
        )

    p_copies, py_copies = [], []

    def project(j):
        vol_copies[j].wait()
        part = jnp.dot(perm[...], vbuf[j], preferred_element_type=F32)
        p_send[j] = part[: 2 * share].astype(BF16)
        copy = remote(p_send.at[j], p_recv.at[j], p_sem.at[0, j], p_sem.at[1, j], mate)
        copy.start()
        p_copies.append(copy)
        p_keep[j] = part[2 * share :]

    def pass_on(j):
        p_copies[j].wait_recv()
        both = p_keep[j] + p_recv[j].astype(F32)
        py_send[j] = both[:share].astype(BF16)
        copy = remote(py_send.at[j], py_recv.at[j], py_sem.at[0, j], py_sem.at[1, j], across)
        copy.start()
        py_copies.append(copy)
        p_keep[j, share:, :] = both[share:]

    project(0)
    w_mate.wait_recv()
    wy_send[...] = (w_keep[...] + w_recv[...].astype(F32)).astype(BF16)
    w_across = remote(wy_send, wy_recv, w_sem.at[2], w_sem.at[3], across)
    w_across.start()
    for j in range(1, pieces):
        project(j)
        pass_on(j - 1)
    pass_on(pieces - 1)

    w_across.wait_recv()
    coef[core] = (wy_send[...].astype(F32) + wy_recv[...].astype(F32)).astype(BF16)
    w_back = remote(coef.at[core], coef.at[core], w_sem.at[4], w_sem.at[5], mate)
    w_back.start()
    remote(coef.at[1 - core], coef.at[1 - core], w_sem.at[4], w_sem.at[5], mate).wait_recv()

    energy = jnp.zeros((1, mode_count), F32)
    for h in range(2):
        for lower in range(0, half, 64):
            value = coef[h, lower : lower + 64, :].astype(F32)
            weight = wcol[h * half + lower : h * half + lower + 64, 0:1]
            energy = energy + jnp.sum(weight * value * value, axis=0, keepdims=True)
    rows = mode_count // LANES
    e_send[...] = jnp.concatenate(
        [energy[:, i * LANES : (i + 1) * LANES] for i in range(rows)]
        + [area_lanes, jnp.zeros((8 - rows - 1, LANES), F32)],
        axis=0,
    )
    e_recv[cell] = e_send[...]
    e_copies = []
    for d, to in enumerate(others):
        copy = remote(e_send, e_recv.at[cell], e_send_sem.at[d], e_recv_sem.at[cell], to)
        copy.start()
        e_copies.append(copy)
    for other in others:
        origin = other[0]
        remote(
            e_send, e_recv.at[origin], e_send_sem.at[0], e_recv_sem.at[origin], other
        ).wait_recv()
    total = jnp.sum(e_recv[...], axis=0)
    area_total = jnp.sum(total[rows : rows + 1, :], axis=1, keepdims=True)
    inverse = lax.rsqrt(total[:rows, :] / area_total + 1e-06)
    inv_row[...] = inverse.reshape(rows, 1, LANES)

    flat = jnp.concatenate([inverse[i : i + 1, :] for i in range(rows)], axis=1)
    for h in range(2):
        for lower in range(0, half, 64):
            at = h * half + lower
            live = lax.broadcasted_iota(jnp.int32, (64, 1), 0) + at < count
            value = coef[h, lower : lower + 64, :].astype(F32) * flat
            wall_buf[at : at + 64, :] = jnp.where(live, value, 0.0).astype(BF16)
    wall_out = pltpu.make_async_copy(wall_buf, wall_ref, out_sem.at[0])
    wall_out.start()

    turned = jnp.broadcast_to(inv_row[y], (LANES, LANES)).T
    inv_col[...] = turned.reshape(2, share, LANES)
    mine = inv_col[core][:, 0:1]
    outs = [wall_out]
    for j in range(pieces):
        py_copies[j].wait_recv()
        summed = p_keep[j, share:, :] + py_recv[j].astype(F32)
        scaled = summed * mass_ref[:, j * width : (j + 1) * width] * mine
        ext_buf[j] = scaled.astype(BF16)
        copy = pltpu.make_async_copy(
            ext_buf.at[j], ext_ref.at[:, pl.ds(j * width, width)], out_sem.at[1 + j]
        )
        copy.start()
        outs.append(copy)

    for copy in sent + [w_mate, w_across, w_back] + p_copies + py_copies + e_copies:
        copy.wait_send()
    for copy in outs:
        copy.wait()


def body(n, temporal_modes, volume_field, mass_root, wall_pressure, face_area, face_count):
    rows, depth = temporal_modes.shape
    mode_count = rows * n
    cells = volume_field.shape[1]
    slots = wall_pressure.shape[0]
    half = slots // 2
    lines = 4
    pieces = 5
    width = cells // pieces
    share = mode_count // 4
    moved = BF16 if rows % 16 == 0 else F32
    group = n // lines
    dma = pltpu.SemaphoreType.DMA
    hbm, vmem, smem = (pl.BlockSpec(memory_space=m) for m in (pl.ANY, pltpu.VMEM, pltpu.SMEM))
    return pl.pallas_call(
        functools.partial(kernel, n, lines, pieces),
        out_shape=(
            jax.ShapeDtypeStruct((share, cells), BF16),
            jax.ShapeDtypeStruct((slots, mode_count), BF16),
        ),
        in_specs=[hbm, hbm, vmem, hbm, vmem, smem],
        out_specs=(hbm, hbm),
        scratch_shapes=[
            pltpu.VMEM((n, rows, depth), moved),
            pltpu.VMEM((mode_count, depth), BF16),
            pltpu.VMEM((pieces, depth, width), BF16),
            pltpu.VMEM((2, half, depth), BF16),
            pltpu.VMEM((slots, LANES), F32),
            pltpu.VMEM((half, mode_count), BF16),
            pltpu.VMEM((half, mode_count), BF16),
            pltpu.VMEM((half, mode_count), F32),
            pltpu.VMEM((half, mode_count), BF16),
            pltpu.VMEM((half, mode_count), BF16),
            pltpu.VMEM((2, half, mode_count), BF16),
            pltpu.VMEM((pieces, 2 * share, width), BF16),
            pltpu.VMEM((pieces, 2 * share, width), BF16),
            pltpu.VMEM((pieces, 2 * share, width), F32),
            pltpu.VMEM((pieces, share, width), BF16),
            pltpu.VMEM((pieces, share, width), BF16),
            pltpu.VMEM((8, LANES), F32),
            pltpu.VMEM((n, 8, LANES), F32),
            pltpu.VMEM((mode_count // LANES, 1, LANES), F32),
            pltpu.VMEM((2, share, LANES), F32),
            pltpu.VMEM((pieces, share, width), BF16),
            pltpu.VMEM((slots, mode_count), BF16),
            dma((3 + pieces,)),
            dma((lines, group - 1 + lines)),
            dma((n,)),
            dma((6,)),
            dma((2, pieces)),
            dma((2, pieces)),
            dma((n,)),
            dma((n,)),
            dma((1 + pieces,)),
        ],
        compiler_params=pltpu.CompilerParams(
            collective_id=0, has_side_effects=True, vmem_limit_bytes=40 * 1024 * 1024
        ),
    )(
        temporal_modes.astype(moved),
        volume_field,
        mass_root.reshape(1, cells),
        wall_pressure,
        face_area.reshape(slots // LANES, LANES),
        face_count,
    )


def solution(mesh):
    in_specs = (
        P("cells", "snap"),
        P("snap", "cells"),
        P("cells"),
        P("cells", "snap"),
        P("cells"),
        P("cells"),
    )
    out_specs = (P("snap", "cells"), P("cells", None))
    return jax.shard_map(
        functools.partial(body, mesh.shape["cells"]),
        mesh=mesh, in_specs=in_specs, out_specs=out_specs, check_vma=False,
    )
```

```python
import functools

import jax
import jax.numpy as jnp
from jax import lax
from jax.experimental import pallas as pl
from jax.experimental.pallas import tpu as pltpu
from jax.sharding import PartitionSpec as P

MESH = pl.DeviceIdType.MESH
F32 = jnp.float32
BF16 = jnp.bfloat16
LANES = 128


def kernel(
    n, lines, pieces,
    modes_ref, vol_ref, mass_ref, press_ref, area_ref, count_ref,
    ext_ref, wall_ref,
    gbuf, perm, vbuf, pbuf, mass, area, wcol,
    w_send, w_recv, w_keep, wy_send, wy_recv, coef,
    p_send, p_recv, p_keep, py_send, py_recv,
    e_send, ex_recv, e_line, ez_recv, inv_row, inv_col,
    load_sem, g_send_sem, g_recv_sem, w_sem, back_sem, p_sem, py_sem, e_send_sem, ex_sem, ez_sem,
):
    cell, snap = lax.axis_index("cells"), lax.axis_index("snap")
    y, core = snap // 2, snap % 2
    group = n // lines
    z, x = cell // group, cell % group
    near = z // 2
    mate = (cell, y * 2 + 1 - core)
    across = (cell, (1 - y) * 2 + core)
    mode_count, depth = perm.shape
    cols = mode_count // 2
    share = mode_count // 4
    per_share = n // 4
    half = pbuf.shape[1]
    width = vbuf.shape[2]
    slots = 2 * half
    parts = gbuf.shape[1]
    part_rows = gbuf.shape[2]

    def remote(src, dst, send, recv, to):
        return pltpu.make_async_remote_copy(
            src_ref=src, dst_ref=dst, send_sem=send, recv_sem=recv,
            device_id=to, device_id_type=MESH,
        )

    pair = near * 2 + 1 - z % 2
    far = [(1 - near) * 2 + z % 2, (1 - near) * 2 + 1 - z % 2]
    along = [at * group + x for at in [pair] + far]
    beside = [z * group + lax.rem(x + d, group) for d in range(1, group)]

    barrier = pltpu.get_barrier_semaphore()
    greeted = [(to, snap) for to in beside + along] + [mate, across]
    for other in greeted:
        pl.semaphore_signal(barrier, inc=1, device_id=other, device_id_type=MESH)

    loads = [
        pltpu.make_async_copy(
            modes_ref.at[pl.ds(i * part_rows, part_rows)], gbuf.at[cell, i], load_sem.at[i]
        )
        for i in range(parts)
    ]
    loads += [
        pltpu.make_async_copy(area_ref, area, load_sem.at[parts]),
        pltpu.make_async_copy(mass_ref, mass, load_sem.at[parts + 1]),
    ]
    press_copies = [
        pltpu.make_async_copy(
            press_ref.at[pl.ds(h * half, half)], pbuf.at[h], load_sem.at[parts + 2 + h]
        )
        for h in range(2)
    ]
    vol_copies = [
        pltpu.make_async_copy(
            vol_ref.at[:, pl.ds(j * width, width)], vbuf.at[j], load_sem.at[parts + 4 + j]
        )
        for j in range(pieces)
    ]
    for copy in loads + press_copies + vol_copies:
        copy.start()

    pl.semaphore_wait(barrier, len(greeted))

    sent = []
    for d, to in enumerate(beside + along):
        for i in range(parts):
            copy = remote(
                modes_ref.at[pl.ds(i * part_rows, part_rows)], gbuf.at[cell, i],
                g_send_sem.at[0, d, i], g_recv_sem.at[cell, i], (to, snap),
            )
            copy.start()
            sent.append(copy)

    def arrived(origin, i, frm):
        remote(
            gbuf.at[origin, i], gbuf.at[origin, i], g_send_sem.at[0, 0, i], g_recv_sem.at[origin, i],
            (frm, snap),
        ).wait_recv()

    def relay(d):
        origin = along[d]
        for i in range(parts):
            arrived(origin, i, origin)
            for e, to in enumerate(beside):
                copy = remote(
                    gbuf.at[origin, i], gbuf.at[origin, i],
                    g_send_sem.at[1 + d, e, i], g_recv_sem.at[origin, i], (to, snap),
                )
                copy.start()
                sent.append(copy)

    def from_side(lines_at):
        for d in range(1, group):
            for at in lines_at:
                for i in range(parts):
                    arrived(at * group + lax.rem(x + d, group), i, z * group + lax.rem(x + d, group))

    def contract(h, modes_half):
        return lax.dot_general(
            pbuf[h], modes_half, (((1,), (1,)), ((), ())), preferred_element_type=F32
        )

    w_mates, w_acrosses = [], []

    def wall(phase, which):
        modes_half = gbuf[pl.ds(which * (n // 2), n // 2)].reshape(cols, depth).astype(BF16)
        w_send[phase] = contract(1 - core, modes_half).astype(BF16)
        copy = remote(
            w_send.at[phase], w_recv.at[phase], w_sem.at[0, phase], w_sem.at[1, phase], mate
        )
        copy.start()
        w_mates.append(copy)
        w_keep[phase] = contract(core, modes_half)

    def wall_pass(phase):
        w_mates[phase].wait_recv()
        wy_send[phase] = (w_keep[phase] + w_recv[phase].astype(F32)).astype(BF16)
        copy = remote(
            wy_send.at[phase], wy_recv.at[phase], w_sem.at[2, phase], w_sem.at[3, phase], across
        )
        copy.start()
        w_acrosses.append(copy)

    def wall_sum(phase, which):
        w_acrosses[phase].wait_recv()
        coef[core, which] = (
            wy_send[phase].astype(F32) + wy_recv[phase].astype(F32)
        ).astype(BF16)

    for copy in loads:
        copy.wait()
    slot_row = lax.broadcasted_iota(jnp.int32, (1, LANES), 1)
    count = count_ref[0]
    area_lanes = jnp.zeros((1, LANES), F32)
    for i in range(slots // LANES):
        row = area[i : i + 1, :].astype(F32)
        row = jnp.where(slot_row + i * LANES < count, row, 0.0)
        area_lanes = area_lanes + row
        wcol[pl.ds(i * LANES, LANES), :] = jnp.broadcast_to(row, (LANES, LANES)).T

    relay(0)
    for copy in press_copies:
        copy.wait()
    from_side([z, pair])
    wall(0, near)
    relay(1)
    wall_pass(0)
    relay(2)
    from_side(far)

    wall(1, 1 - near)

    order = [
        (1 - y) * 2 + 1 - core, y * 2 + 1 - core, (1 - y) * 2 + core, y * 2 + core,
    ]
    for i, s in enumerate(order):
        perm[pl.ds(i * share, share), :] = (
            gbuf[pl.ds(s * per_share, per_share)].reshape(share, depth).astype(BF16)
        )

    p_copies, py_copies = [], []

    def project(j):
        vol_copies[j].wait()
        part = jnp.dot(perm[...], vbuf[j], preferred_element_type=F32)
        p_send[j] = part[: 2 * share].astype(BF16)
        copy = remote(p_send.at[j], p_recv.at[j], p_sem.at[0, j], p_sem.at[1, j], mate)
        copy.start()
        p_copies.append(copy)
        p_keep[j] = part[2 * share :]

    def pass_on(j):
        p_copies[j].wait_recv()
        both = p_keep[j] + p_recv[j].astype(F32)
        py_send[j] = both[:share].astype(BF16)
        copy = remote(py_send.at[j], py_recv.at[j], py_sem.at[0, j], py_sem.at[1, j], across)
        copy.start()
        py_copies.append(copy)
        p_keep[j, share:, :] = both[share:]

    project(0)
    wall_pass(1)
    for j in range(1, pieces):
        project(j)
        pass_on(j - 1)
    pass_on(pieces - 1)

    wall_sum(0, near)
    wall_sum(1, 1 - near)
    w_back = remote(coef.at[core], coef.at[core], back_sem.at[0], back_sem.at[1], mate)
    w_back.start()
    remote(coef.at[1 - core], coef.at[1 - core], back_sem.at[0], back_sem.at[1], mate).wait_recv()

    rows = mode_count // LANES
    each = cols // LANES
    energy = [jnp.zeros((1, cols), F32) for _ in range(2)]
    for h in range(2):
        for lower in range(0, half, 64):
            weight = wcol[h * half + lower : h * half + lower + 64, 0:1]
            for m in range(2):
                value = coef[h, m, lower : lower + 64, :].astype(F32)
                energy[m] = energy[m] + jnp.sum(weight * value * value, axis=0, keepdims=True)
    e_send[...] = jnp.concatenate(
        [energy[i // each][:, (i % each) * LANES : (i % each + 1) * LANES] for i in range(rows)]
        + [area_lanes, jnp.zeros((8 - rows - 1, LANES), F32)],
        axis=0,
    )
    e_copies = []

    def gather_sum(src, slots_ref, at, sems, base, peers):
        slots_ref[at] = src[...]
        for d, (to, _) in enumerate(peers):
            copy = remote(src, slots_ref.at[at], e_send_sem.at[base + d], sems.at[at], (to, snap))
            copy.start()
            e_copies.append(copy)
        for to, slot in peers:
            remote(
                src, slots_ref.at[slot], e_send_sem.at[base], sems.at[slot], (to, snap)
            ).wait_recv()
        return jnp.sum(slots_ref[...], axis=0)

    e_line[...] = gather_sum(
        e_send, ex_recv, x, ex_sem, 0,
        [(to, lax.rem(x + 1 + d, group)) for d, to in enumerate(beside)],
    )
    total = gather_sum(
        e_line, ez_recv, z, ez_sem, group - 1, list(zip(along, [pair] + far))
    )
    area_total = jnp.sum(total[rows : rows + 1, :], axis=1, keepdims=True)
    inverse = lax.rsqrt(total[:rows, :] / area_total + 1e-06)
    inv_row[...] = inverse.reshape(rows, 1, LANES)

    for m in range(2):
        flat = jnp.concatenate([inverse[i : i + 1, :] for i in range(m * each, (m + 1) * each)], axis=1)
        for h in range(2):
            for lower in range(0, half, 64):
                at = h * half + lower
                live = lax.broadcasted_iota(jnp.int32, (64, 1), 0) + at < count
                value = coef[h, m, lower : lower + 64, :].astype(F32) * flat
                wall_ref[at : at + 64, m * cols : (m + 1) * cols] = jnp.where(
                    live, value, 0.0
                ).astype(BF16)

    turned = jnp.broadcast_to(inv_row[y], (LANES, LANES)).T
    inv_col[...] = turned.reshape(2, share, LANES)
    mine = inv_col[core]
    for j in range(pieces):
        py_copies[j].wait_recv()
        for i in range(width // LANES):
            at = slice(i * LANES, (i + 1) * LANES)
            row = j * (width // LANES) + i
            summed = p_keep[j, share:, at] + py_recv[j, :, at].astype(F32)
            scaled = summed * mass[row : row + 1, :] * mine
            ext_ref[:, row * LANES : (row + 1) * LANES] = scaled.astype(BF16)

    for copy in sent + w_mates + w_acrosses + [w_back] + p_copies + py_copies + e_copies:
        copy.wait_send()


def deliver(ext_in, wall_in, ext_out, wall_out, sems):
    copies = [
        pltpu.make_async_copy(ext_in, ext_out, sems.at[0]),
        pltpu.make_async_copy(wall_in, wall_out, sems.at[1]),
    ]
    for copy in copies:
        copy.start()
    for copy in copies:
        copy.wait()


def body(n, temporal_modes, volume_field, mass_root, wall_pressure, face_area, face_count):
    rows, depth = temporal_modes.shape
    mode_count = rows * n
    cells = volume_field.shape[1]
    slots = wall_pressure.shape[0]
    half = slots // 2
    lines = 4
    pieces = 5
    width = cells // pieces
    share = mode_count // 4
    cols = mode_count // 2
    moved = BF16 if rows % 16 == 0 else F32
    parts = 2 if rows % 32 == 0 else 1
    group = n // lines
    dma = pltpu.SemaphoreType.DMA
    hbm, vmem, smem, anywhere = (
        pl.BlockSpec(memory_space=m) for m in (pltpu.HBM, pltpu.VMEM, pltpu.SMEM, pl.ANY)
    )
    shapes = (
        jax.ShapeDtypeStruct((share, cells), BF16),
        jax.ShapeDtypeStruct((slots, mode_count), BF16),
    )
    results = pl.pallas_call(
        functools.partial(kernel, n, lines, pieces),
        out_shape=tuple(pltpu.VMEM(s.shape, s.dtype) for s in shapes),
        in_specs=[hbm] * 5 + [smem],
        out_specs=(vmem, vmem),
        scratch_shapes=[
            pltpu.VMEM((n, parts, rows // parts, depth), moved),
            pltpu.VMEM((mode_count, depth), BF16),
            pltpu.VMEM((pieces, depth, width), BF16),
            pltpu.VMEM((2, half, depth), BF16),
            pltpu.VMEM((cells // LANES, LANES), F32),
            pltpu.VMEM((slots // LANES, LANES), BF16),
            pltpu.VMEM((slots, LANES), F32),
            pltpu.VMEM((2, half, cols), BF16),
            pltpu.VMEM((2, half, cols), BF16),
            pltpu.VMEM((2, half, cols), F32),
            pltpu.VMEM((2, half, cols), BF16),
            pltpu.VMEM((2, half, cols), BF16),
            pltpu.VMEM((2, 2, half, cols), BF16),
            pltpu.VMEM((pieces, 2 * share, width), BF16),
            pltpu.VMEM((pieces, 2 * share, width), BF16),
            pltpu.VMEM((pieces, 2 * share, width), F32),
            pltpu.VMEM((pieces, share, width), BF16),
            pltpu.VMEM((pieces, share, width), BF16),
            pltpu.VMEM((8, LANES), F32),
            pltpu.VMEM((group, 8, LANES), F32),
            pltpu.VMEM((8, LANES), F32),
            pltpu.VMEM((lines, 8, LANES), F32),
            pltpu.VMEM((mode_count // LANES, 1, LANES), F32),
            pltpu.VMEM((2, share, LANES), F32),
            dma((parts + 4 + pieces,)),
            dma((lines, group - 1 + lines - 1, parts)),
            dma((n, parts)),
            dma((4, 2)),
            dma((2,)),
            dma((2, pieces)),
            dma((2, pieces)),
            dma((group - 1 + lines - 1,)),
            dma((group,)),
            dma((lines,)),
        ],
        compiler_params=pltpu.CompilerParams(
            collective_id=0, has_side_effects=True, vmem_limit_bytes=58 * 1024 * 1024
        ),
    )(
        temporal_modes.astype(moved),
        volume_field,
        mass_root.reshape(cells // LANES, LANES),
        wall_pressure,
        face_area.reshape(slots // LANES, LANES),
        face_count,
    )
    return pl.pallas_call(
        deliver,
        out_shape=shapes,
        in_specs=[vmem, vmem],
        out_specs=(anywhere, anywhere),
        scratch_shapes=[dma((2,))],
        compiler_params=pltpu.CompilerParams(vmem_limit_bytes=1024 * 1024),
    )(*results)


def solution(mesh):
    in_specs = (
        P("cells", "snap"),
        P("snap", "cells"),
        P("cells"),
        P("cells", "snap"),
        P("cells"),
        P("cells"),
    )
    out_specs = (P("snap", "cells"), P("cells", None))
    return jax.shard_map(
        functools.partial(body, mesh.shape["cells"]),
        mesh=mesh, in_specs=in_specs, out_specs=out_specs, check_vma=False,
    )
```

```python
import functools

import jax
import jax.numpy as jnp
from jax import lax
from jax.experimental import pallas as pl
from jax.experimental.pallas import tpu as pltpu
from jax.sharding import PartitionSpec as P

MESH = pl.DeviceIdType.MESH
F32 = jnp.float32
BF16 = jnp.bfloat16
LANES = 128


def kernel(
    n, lines, pieces,
    modes_ref, vol_ref, mass_ref, press_ref, area_ref, count_ref,
    ext_ref, wall_ref,
    gbuf, perm, vbuf, pbuf, mass, area, wcol,
    w_send, w_recv, w_keep, wy_send, wy_recv, coef,
    p_send, p_recv, p_keep, py_send, py_recv,
    e_send, ex_recv, e_line, ez_recv, inv_row, inv_col,
    load_sem, g_send_sem, g_recv_sem, w_sem, back_sem, p_sem, py_sem, e_send_sem, ex_sem, ez_sem,
):
    cell, snap = lax.axis_index("cells"), lax.axis_index("snap")
    y, core = snap // 2, snap % 2
    group = n // lines
    z, x = cell // group, cell % group
    near = z // 2
    mate = (cell, y * 2 + 1 - core)
    across = (cell, (1 - y) * 2 + core)
    mode_count, depth = perm.shape
    cols = mode_count // 2
    share = mode_count // 4
    per_share = n // 4
    half = pbuf.shape[1]
    width = vbuf.shape[2]
    slots = 2 * half
    parts = gbuf.shape[1]
    part_rows = gbuf.shape[2]

    def remote(src, dst, send, recv, to):
        return pltpu.make_async_remote_copy(
            src_ref=src, dst_ref=dst, send_sem=send, recv_sem=recv,
            device_id=to, device_id_type=MESH,
        )

    pair = near * 2 + 1 - z % 2
    far = [(1 - near) * 2 + z % 2, (1 - near) * 2 + 1 - z % 2]
    along = [at * group + x for at in [pair] + far]
    beside = [z * group + lax.rem(x + d, group) for d in range(1, group)]

    barrier = pltpu.get_barrier_semaphore()
    greeted = [(to, snap) for to in beside + along] + [mate, across]
    for other in greeted:
        pl.semaphore_signal(barrier, inc=1, device_id=other, device_id_type=MESH)

    loads = [
        pltpu.make_async_copy(
            modes_ref.at[pl.ds(i * part_rows, part_rows)], gbuf.at[cell, i], load_sem.at[i]
        )
        for i in range(parts)
    ]
    loads += [
        pltpu.make_async_copy(area_ref, area, load_sem.at[parts]),
        pltpu.make_async_copy(mass_ref, mass, load_sem.at[parts + 1]),
    ]
    press_copies = [
        pltpu.make_async_copy(
            press_ref.at[pl.ds(h * half, half)], pbuf.at[h], load_sem.at[parts + 2 + h]
        )
        for h in range(2)
    ]
    vol_copies = [
        pltpu.make_async_copy(
            vol_ref.at[:, pl.ds(j * width, width)], vbuf.at[j], load_sem.at[parts + 4 + j]
        )
        for j in range(pieces)
    ]
    for copy in loads + press_copies + vol_copies:
        copy.start()

    pl.semaphore_wait(barrier, len(greeted))

    sent = []
    for d, to in enumerate(beside + along[1:] + along[:1]):
        for i in range(parts):
            copy = remote(
                modes_ref.at[pl.ds(i * part_rows, part_rows)], gbuf.at[cell, i],
                g_send_sem.at[0, d, i], g_recv_sem.at[cell, i], (to, snap),
            )
            copy.start()
            sent.append(copy)

    def arrived(origin, i, frm):
        remote(
            gbuf.at[origin, i], gbuf.at[origin, i], g_send_sem.at[0, 0, i], g_recv_sem.at[origin, i],
            (frm, snap),
        ).wait_recv()

    def relay(d):
        origin = along[d]
        for i in range(parts):
            arrived(origin, i, origin)
            for e, to in enumerate(beside):
                copy = remote(
                    gbuf.at[origin, i], gbuf.at[origin, i],
                    g_send_sem.at[1 + d, e, i], g_recv_sem.at[origin, i], (to, snap),
                )
                copy.start()
                sent.append(copy)

    def from_side(lines_at):
        for d in range(1, group):
            for at in lines_at:
                for i in range(parts):
                    arrived(at * group + lax.rem(x + d, group), i, z * group + lax.rem(x + d, group))

    def contract(h, modes_half):
        return lax.dot_general(
            pbuf[h], modes_half, (((1,), (1,)), ((), ())), preferred_element_type=F32
        )

    w_mates, w_acrosses = [], []

    def wall(phase, which):
        modes_half = gbuf[pl.ds(which * (n // 2), n // 2)].reshape(cols, depth).astype(BF16)
        w_send[phase] = contract(1 - core, modes_half).astype(BF16)
        copy = remote(
            w_send.at[phase], w_recv.at[phase], w_sem.at[0, phase], w_sem.at[1, phase], mate
        )
        copy.start()
        w_mates.append(copy)
        w_keep[phase] = contract(core, modes_half)

    def wall_pass(phase):
        w_mates[phase].wait_recv()
        wy_send[phase] = (w_keep[phase] + w_recv[phase].astype(F32)).astype(BF16)
        copy = remote(
            wy_send.at[phase], wy_recv.at[phase], w_sem.at[2, phase], w_sem.at[3, phase], across
        )
        copy.start()
        w_acrosses.append(copy)

    def wall_sum(phase, which):
        w_acrosses[phase].wait_recv()
        coef[core, which] = (
            wy_send[phase].astype(F32) + wy_recv[phase].astype(F32)
        ).astype(BF16)

    for copy in loads:
        copy.wait()
    slot_row = lax.broadcasted_iota(jnp.int32, (1, LANES), 1)
    count = count_ref[0]
    area_lanes = jnp.zeros((1, LANES), F32)
    for i in range(slots // LANES):
        row = area[i : i + 1, :].astype(F32)
        row = jnp.where(slot_row + i * LANES < count, row, 0.0)
        area_lanes = area_lanes + row
        wcol[pl.ds(i * LANES, LANES), :] = jnp.broadcast_to(row, (LANES, LANES)).T

    relay(1)
    relay(0)
    relay(2)
    for copy in press_copies:
        copy.wait()
    from_side([z, pair])
    wall(0, near)
    wall_pass(0)
    from_side(far)

    wall(1, 1 - near)

    order = [
        (1 - y) * 2 + 1 - core, y * 2 + 1 - core, (1 - y) * 2 + core, y * 2 + core,
    ]
    for i, s in enumerate(order):
        perm[pl.ds(i * share, share), :] = (
            gbuf[pl.ds(s * per_share, per_share)].reshape(share, depth).astype(BF16)
        )

    p_copies, py_copies = [], []

    def project(j):
        vol_copies[j].wait()
        part = jnp.dot(perm[...], vbuf[j], preferred_element_type=F32)
        p_send[j] = part[: 2 * share].astype(BF16)
        copy = remote(p_send.at[j], p_recv.at[j], p_sem.at[0, j], p_sem.at[1, j], mate)
        copy.start()
        p_copies.append(copy)
        p_keep[j] = part[2 * share :]

    def pass_on(j):
        p_copies[j].wait_recv()
        both = p_keep[j] + p_recv[j].astype(F32)
        py_send[j] = both[:share].astype(BF16)
        copy = remote(py_send.at[j], py_recv.at[j], py_sem.at[0, j], py_sem.at[1, j], across)
        copy.start()
        py_copies.append(copy)
        p_keep[j, share:, :] = both[share:]

    project(0)
    wall_pass(1)
    for j in range(1, pieces):
        project(j)
        pass_on(j - 1)
    pass_on(pieces - 1)

    wall_sum(0, near)
    wall_sum(1, 1 - near)
    w_back = remote(coef.at[core], coef.at[core], back_sem.at[0], back_sem.at[1], mate)
    w_back.start()
    remote(coef.at[1 - core], coef.at[1 - core], back_sem.at[0], back_sem.at[1], mate).wait_recv()

    rows = mode_count // LANES
    each = cols // LANES
    energy = [jnp.zeros((1, cols), F32) for _ in range(2)]
    for h in range(2):
        for lower in range(0, half, 64):
            weight = wcol[h * half + lower : h * half + lower + 64, 0:1]
            for m in range(2):
                value = coef[h, m, lower : lower + 64, :].astype(F32)
                energy[m] = energy[m] + jnp.sum(weight * value * value, axis=0, keepdims=True)
    e_send[...] = jnp.concatenate(
        [energy[i // each][:, (i % each) * LANES : (i % each + 1) * LANES] for i in range(rows)]
        + [area_lanes, jnp.zeros((8 - rows - 1, LANES), F32)],
        axis=0,
    )
    e_copies = []

    def gather_sum(src, slots_ref, at, sems, base, peers):
        slots_ref[at] = src[...]
        for d, (to, _) in enumerate(peers):
            copy = remote(src, slots_ref.at[at], e_send_sem.at[base + d], sems.at[at], (to, snap))
            copy.start()
            e_copies.append(copy)
        for to, slot in peers:
            remote(
                src, slots_ref.at[slot], e_send_sem.at[base], sems.at[slot], (to, snap)
            ).wait_recv()
        return jnp.sum(slots_ref[...], axis=0)

    e_line[...] = gather_sum(
        e_send, ex_recv, x, ex_sem, 0,
        [(to, lax.rem(x + 1 + d, group)) for d, to in enumerate(beside)],
    )
    total = gather_sum(
        e_line, ez_recv, z, ez_sem, group - 1, list(zip(along, [pair] + far))
    )
    area_total = jnp.sum(total[rows : rows + 1, :], axis=1, keepdims=True)
    inverse = lax.rsqrt(total[:rows, :] / area_total + 1e-06)
    inv_row[...] = inverse.reshape(rows, 1, LANES)

    for m in range(2):
        flat = jnp.concatenate([inverse[i : i + 1, :] for i in range(m * each, (m + 1) * each)], axis=1)
        for h in range(2):
            for lower in range(0, half, 64):
                at = h * half + lower
                live = lax.broadcasted_iota(jnp.int32, (64, 1), 0) + at < count
                value = coef[h, m, lower : lower + 64, :].astype(F32) * flat
                wall_ref[at : at + 64, m * cols : (m + 1) * cols] = jnp.where(
                    live, value, 0.0
                ).astype(BF16)

    turned = jnp.broadcast_to(inv_row[y], (LANES, LANES)).T
    inv_col[...] = turned.reshape(2, share, LANES)
    mine = inv_col[core]
    for j in range(pieces):
        py_copies[j].wait_recv()
        for i in range(width // LANES):
            at = slice(i * LANES, (i + 1) * LANES)
            row = j * (width // LANES) + i
            summed = p_keep[j, share:, at] + py_recv[j, :, at].astype(F32)
            scaled = summed * mass[row : row + 1, :] * mine
            ext_ref[:, row * LANES : (row + 1) * LANES] = scaled.astype(BF16)

    for copy in sent + w_mates + w_acrosses + [w_back] + p_copies + py_copies + e_copies:
        copy.wait_send()


def deliver(ext_in, wall_in, ext_out, wall_out, sems):
    copies = [
        pltpu.make_async_copy(ext_in, ext_out, sems.at[0]),
        pltpu.make_async_copy(wall_in, wall_out, sems.at[1]),
    ]
    for copy in copies:
        copy.start()
    for copy in copies:
        copy.wait()


def body(n, temporal_modes, volume_field, mass_root, wall_pressure, face_area, face_count):
    rows, depth = temporal_modes.shape
    mode_count = rows * n
    cells = volume_field.shape[1]
    slots = wall_pressure.shape[0]
    half = slots // 2
    lines = 4
    pieces = 4
    width = cells // pieces
    share = mode_count // 4
    cols = mode_count // 2
    moved = BF16 if rows % 16 == 0 else F32
    parts = 2 if rows % 32 == 0 else 1
    group = n // lines
    dma = pltpu.SemaphoreType.DMA
    hbm, vmem, smem, anywhere = (
        pl.BlockSpec(memory_space=m) for m in (pltpu.HBM, pltpu.VMEM, pltpu.SMEM, pl.ANY)
    )
    shapes = (
        jax.ShapeDtypeStruct((share, cells), BF16),
        jax.ShapeDtypeStruct((slots, mode_count), BF16),
    )
    results = pl.pallas_call(
        functools.partial(kernel, n, lines, pieces),
        out_shape=tuple(pltpu.VMEM(s.shape, s.dtype) for s in shapes),
        in_specs=[hbm] * 5 + [smem],
        out_specs=(vmem, vmem),
        scratch_shapes=[
            pltpu.VMEM((n, parts, rows // parts, depth), moved),
            pltpu.VMEM((mode_count, depth), BF16),
            pltpu.VMEM((pieces, depth, width), BF16),
            pltpu.VMEM((2, half, depth), BF16),
            pltpu.VMEM((cells // LANES, LANES), F32),
            pltpu.VMEM((slots // LANES, LANES), BF16),
            pltpu.VMEM((slots, LANES), F32),
            pltpu.VMEM((2, half, cols), BF16),
            pltpu.VMEM((2, half, cols), BF16),
            pltpu.VMEM((2, half, cols), F32),
            pltpu.VMEM((2, half, cols), BF16),
            pltpu.VMEM((2, half, cols), BF16),
            pltpu.VMEM((2, 2, half, cols), BF16),
            pltpu.VMEM((pieces, 2 * share, width), BF16),
            pltpu.VMEM((pieces, 2 * share, width), BF16),
            pltpu.VMEM((pieces, 2 * share, width), F32),
            pltpu.VMEM((pieces, share, width), BF16),
            pltpu.VMEM((pieces, share, width), BF16),
            pltpu.VMEM((8, LANES), F32),
            pltpu.VMEM((group, 8, LANES), F32),
            pltpu.VMEM((8, LANES), F32),
            pltpu.VMEM((lines, 8, LANES), F32),
            pltpu.VMEM((mode_count // LANES, 1, LANES), F32),
            pltpu.VMEM((2, share, LANES), F32),
            dma((parts + 4 + pieces,)),
            dma((lines, group - 1 + lines - 1, parts)),
            dma((n, parts)),
            dma((4, 2)),
            dma((2,)),
            dma((2, pieces)),
            dma((2, pieces)),
            dma((group - 1 + lines - 1,)),
            dma((group,)),
            dma((lines,)),
        ],
        compiler_params=pltpu.CompilerParams(
            collective_id=0, has_side_effects=True, vmem_limit_bytes=58 * 1024 * 1024
        ),
    )(
        temporal_modes.astype(moved),
        volume_field,
        mass_root.reshape(cells // LANES, LANES),
        wall_pressure,
        face_area.reshape(slots // LANES, LANES),
        face_count,
    )
    return pl.pallas_call(
        deliver,
        out_shape=shapes,
        in_specs=[vmem, vmem],
        out_specs=(anywhere, anywhere),
        scratch_shapes=[dma((2,))],
        compiler_params=pltpu.CompilerParams(vmem_limit_bytes=1024 * 1024),
    )(*results)


def solution(mesh):
    in_specs = (
        P("cells", "snap"),
        P("snap", "cells"),
        P("cells"),
        P("cells", "snap"),
        P("cells"),
        P("cells"),
    )
    out_specs = (P("snap", "cells"), P("cells", None))
    return jax.shard_map(
        functools.partial(body, mesh.shape["cells"]),
        mesh=mesh, in_specs=in_specs, out_specs=out_specs, check_vma=False,
    )
```

```python
import functools

import jax
import jax.numpy as jnp
from jax import lax
from jax.experimental import pallas as pl
from jax.experimental.pallas import tpu as pltpu
from jax.sharding import PartitionSpec as P

MESH = pl.DeviceIdType.MESH
F32 = jnp.float32
BF16 = jnp.bfloat16
LANES = 128


def kernel(
    n, lines, pieces,
    modes_ref, vol_ref, mass_ref, press_ref, area_ref, count_ref,
    ext_ref, wall_ref,
    gbuf, perm, vbuf, pbuf, mass, area, wcol,
    w_send, w_recv, w_keep, wy_send, wy_recv, coef,
    p_send, p_recv, p_keep, py_send, py_recv,
    e_send, ex_recv, e_line, ez_recv, inv_row, inv_col,
    load_sem, g_send_sem, g_recv_sem, w_sem, back_sem, p_sem, py_sem, e_send_sem, ex_sem, ez_sem,
):
    cell, snap = lax.axis_index("cells"), lax.axis_index("snap")
    y, core = snap // 2, snap % 2
    group = n // lines
    z, x = cell // group, cell % group
    near = z // 2
    mate = (cell, y * 2 + 1 - core)
    across = (cell, (1 - y) * 2 + core)
    mode_count, depth = perm.shape
    cols = mode_count // 2
    share = mode_count // 4
    per_share = n // 4
    half = pbuf.shape[1]
    width = vbuf.shape[2]
    slots = 2 * half
    parts = gbuf.shape[1]
    part_rows = gbuf.shape[2]

    def remote(src, dst, send, recv, to):
        return pltpu.make_async_remote_copy(
            src_ref=src, dst_ref=dst, send_sem=send, recv_sem=recv,
            device_id=to, device_id_type=MESH,
        )

    pair = near * 2 + 1 - z % 2
    far = [(1 - near) * 2 + z % 2, (1 - near) * 2 + 1 - z % 2]
    along = [at * group + x for at in [pair] + far]
    beside = [z * group + lax.rem(x + d, group) for d in range(1, group)]

    barrier = pltpu.get_barrier_semaphore()
    greeted = [(to, snap) for to in beside + along] + [mate, across]
    for other in greeted:
        pl.semaphore_signal(barrier, inc=1, device_id=other, device_id_type=MESH)

    loads = [
        pltpu.make_async_copy(
            modes_ref.at[pl.ds(i * part_rows, part_rows)], gbuf.at[cell, i], load_sem.at[i]
        )
        for i in range(parts)
    ]
    loads += [
        pltpu.make_async_copy(area_ref, area, load_sem.at[parts]),
        pltpu.make_async_copy(mass_ref, mass, load_sem.at[parts + 1]),
    ]
    press_copies = [
        pltpu.make_async_copy(
            press_ref.at[pl.ds(h * half, half)], pbuf.at[h], load_sem.at[parts + 2 + h]
        )
        for h in range(2)
    ]
    vol_copies = [
        pltpu.make_async_copy(
            vol_ref.at[:, pl.ds(j * width, width)], vbuf.at[j], load_sem.at[parts + 4 + j]
        )
        for j in range(pieces)
    ]
    for copy in loads + press_copies + vol_copies:
        copy.start()

    pl.semaphore_wait(barrier, len(greeted))

    sent = []
    for d, to in enumerate(beside + along[1:] + along[:1]):
        for i in range(parts):
            copy = remote(
                modes_ref.at[pl.ds(i * part_rows, part_rows)], gbuf.at[cell, i],
                g_send_sem.at[0, d, i], g_recv_sem.at[cell, i], (to, snap),
            )
            copy.start()
            sent.append(copy)

    def arrived(origin, i, frm):
        remote(
            gbuf.at[origin, i], gbuf.at[origin, i], g_send_sem.at[0, 0, i], g_recv_sem.at[origin, i],
            (frm, snap),
        ).wait_recv()

    def relay(d):
        origin = along[d]
        for i in range(parts):
            arrived(origin, i, origin)
            for e, to in enumerate(beside):
                copy = remote(
                    gbuf.at[origin, i], gbuf.at[origin, i],
                    g_send_sem.at[1 + d, e, i], g_recv_sem.at[origin, i], (to, snap),
                )
                copy.start()
                sent.append(copy)

    def from_side(lines_at):
        for d in range(1, group):
            for at in lines_at:
                for i in range(parts):
                    arrived(at * group + lax.rem(x + d, group), i, z * group + lax.rem(x + d, group))

    def contract(h, modes_half):
        return lax.dot_general(
            pbuf[h], modes_half, (((1,), (1,)), ((), ())), preferred_element_type=F32
        )

    w_mates, w_acrosses = [], []

    def wall(phase, which):
        modes_half = gbuf[pl.ds(which * (n // 2), n // 2)].reshape(cols, depth).astype(BF16)
        w_send[phase] = contract(1 - core, modes_half).astype(BF16)
        copy = remote(
            w_send.at[phase], w_recv.at[phase], w_sem.at[0, phase], w_sem.at[1, phase], mate
        )
        copy.start()
        w_mates.append(copy)
        w_keep[phase] = contract(core, modes_half)

    def wall_pass(phase):
        w_mates[phase].wait_recv()
        wy_send[phase] = (w_keep[phase] + w_recv[phase].astype(F32)).astype(BF16)
        copy = remote(
            wy_send.at[phase], wy_recv.at[phase], w_sem.at[2, phase], w_sem.at[3, phase], across
        )
        copy.start()
        w_acrosses.append(copy)

    def wall_sum(phase, which):
        w_acrosses[phase].wait_recv()
        coef[core, which] = (
            wy_send[phase].astype(F32) + wy_recv[phase].astype(F32)
        ).astype(BF16)

    for copy in loads:
        copy.wait()
    slot_row = lax.broadcasted_iota(jnp.int32, (1, LANES), 1)
    count = count_ref[0]
    area_lanes = jnp.zeros((1, LANES), F32)
    for i in range(slots // LANES):
        row = area[i : i + 1, :].astype(F32)
        row = jnp.where(slot_row + i * LANES < count, row, 0.0)
        area_lanes = area_lanes + row
        wcol[pl.ds(i * LANES, LANES), :] = jnp.broadcast_to(row, (LANES, LANES)).T

    relay(1)
    relay(0)
    relay(2)
    for copy in press_copies:
        copy.wait()
    from_side([z, pair])
    wall(0, near)
    wall_pass(0)
    from_side(far)

    wall(1, 1 - near)

    order = [
        (1 - y) * 2 + 1 - core, y * 2 + 1 - core, (1 - y) * 2 + core, y * 2 + core,
    ]
    for i, s in enumerate(order):
        perm[pl.ds(i * share, share), :] = (
            gbuf[pl.ds(s * per_share, per_share)].reshape(share, depth).astype(BF16)
        )

    p_copies, py_copies = [], []

    def project(j):
        vol_copies[j].wait()
        part = jnp.dot(perm[...], vbuf[j], preferred_element_type=F32)
        p_send[j] = part[: 2 * share].astype(BF16)
        copy = remote(p_send.at[j], p_recv.at[j], p_sem.at[0, j], p_sem.at[1, j], mate)
        copy.start()
        p_copies.append(copy)
        p_keep[j] = part[2 * share :]

    def pass_on(j):
        p_copies[j].wait_recv()
        both = p_keep[j] + p_recv[j].astype(F32)
        py_send[j] = both[:share].astype(BF16)
        copy = remote(py_send.at[j], py_recv.at[j], py_sem.at[0, j], py_sem.at[1, j], across)
        copy.start()
        py_copies.append(copy)
        p_keep[j, share:, :] = both[share:]

    def wall_back():
        wall_sum(0, near)
        wall_sum(1, 1 - near)
        copy = remote(coef.at[core], coef.at[core], back_sem.at[0], back_sem.at[1], mate)
        copy.start()
        return copy

    project(0)
    wall_pass(1)
    for j in range(1, pieces):
        project(j)
        pass_on(j - 1)
    w_back = wall_back()
    pass_on(pieces - 1)


    remote(coef.at[1 - core], coef.at[1 - core], back_sem.at[0], back_sem.at[1], mate).wait_recv()

    rows = mode_count // LANES
    each = cols // LANES
    energy = [jnp.zeros((1, cols), F32) for _ in range(2)]
    for h in range(2):
        for lower in range(0, half, 64):
            weight = wcol[h * half + lower : h * half + lower + 64, 0:1]
            for m in range(2):
                value = coef[h, m, lower : lower + 64, :].astype(F32)
                energy[m] = energy[m] + jnp.sum(weight * value * value, axis=0, keepdims=True)
    e_send[...] = jnp.concatenate(
        [energy[i // each][:, (i % each) * LANES : (i % each + 1) * LANES] for i in range(rows)]
        + [area_lanes, jnp.zeros((8 - rows - 1, LANES), F32)],
        axis=0,
    )
    e_copies = []

    def gather_sum(src, slots_ref, at, sems, base, peers):
        slots_ref[at] = src[...]
        for d, (to, _) in enumerate(peers):
            copy = remote(src, slots_ref.at[at], e_send_sem.at[base + d], sems.at[at], (to, snap))
            copy.start()
            e_copies.append(copy)
        for to, slot in peers:
            remote(
                src, slots_ref.at[slot], e_send_sem.at[base], sems.at[slot], (to, snap)
            ).wait_recv()
        return jnp.sum(slots_ref[...], axis=0)

    e_line[...] = gather_sum(
        e_send, ex_recv, x, ex_sem, 0,
        [(to, lax.rem(x + 1 + d, group)) for d, to in enumerate(beside)],
    )
    total = gather_sum(
        e_line, ez_recv, z, ez_sem, group - 1, list(zip(along, [pair] + far))
    )
    area_total = jnp.sum(total[rows : rows + 1, :], axis=1, keepdims=True)
    inverse = lax.rsqrt(total[:rows, :] / area_total + 1e-06)
    inv_row[...] = inverse.reshape(rows, 1, LANES)

    for m in range(2):
        flat = jnp.concatenate([inverse[i : i + 1, :] for i in range(m * each, (m + 1) * each)], axis=1)
        for h in range(2):
            for lower in range(0, half, 64):
                at = h * half + lower
                live = lax.broadcasted_iota(jnp.int32, (64, 1), 0) + at < count
                value = coef[h, m, lower : lower + 64, :].astype(F32) * flat
                wall_ref[at : at + 64, m * cols : (m + 1) * cols] = jnp.where(
                    live, value, 0.0
                ).astype(BF16)

    turned = jnp.broadcast_to(inv_row[y], (LANES, LANES)).T
    inv_col[...] = turned.reshape(2, share, LANES)
    mine = inv_col[core]
    for j in range(pieces):
        py_copies[j].wait_recv()
        for i in range(width // LANES):
            at = slice(i * LANES, (i + 1) * LANES)
            row = j * (width // LANES) + i
            summed = p_keep[j, share:, at] + py_recv[j, :, at].astype(F32)
            scaled = summed * mass[row : row + 1, :] * mine
            ext_ref[:, row * LANES : (row + 1) * LANES] = scaled.astype(BF16)

    for copy in sent + w_mates + w_acrosses + [w_back] + p_copies + py_copies + e_copies:
        copy.wait_send()


def deliver(ext_in, wall_in, ext_out, wall_out, sems):
    copies = [
        pltpu.make_async_copy(ext_in, ext_out, sems.at[0]),
        pltpu.make_async_copy(wall_in, wall_out, sems.at[1]),
    ]
    for copy in copies:
        copy.start()
    for copy in copies:
        copy.wait()


def body(n, temporal_modes, volume_field, mass_root, wall_pressure, face_area, face_count):
    rows, depth = temporal_modes.shape
    mode_count = rows * n
    cells = volume_field.shape[1]
    slots = wall_pressure.shape[0]
    half = slots // 2
    lines = 4
    pieces = 4
    width = cells // pieces
    share = mode_count // 4
    cols = mode_count // 2
    moved = BF16 if rows % 16 == 0 else F32
    parts = 2 if rows % 32 == 0 else 1
    group = n // lines
    dma = pltpu.SemaphoreType.DMA
    hbm, vmem, smem, anywhere = (
        pl.BlockSpec(memory_space=m) for m in (pltpu.HBM, pltpu.VMEM, pltpu.SMEM, pl.ANY)
    )
    shapes = (
        jax.ShapeDtypeStruct((share, cells), BF16),
        jax.ShapeDtypeStruct((slots, mode_count), BF16),
    )
    results = pl.pallas_call(
        functools.partial(kernel, n, lines, pieces),
        out_shape=tuple(pltpu.VMEM(s.shape, s.dtype) for s in shapes),
        in_specs=[hbm] * 5 + [smem],
        out_specs=(vmem, vmem),
        scratch_shapes=[
            pltpu.VMEM((n, parts, rows // parts, depth), moved),
            pltpu.VMEM((mode_count, depth), BF16),
            pltpu.VMEM((pieces, depth, width), BF16),
            pltpu.VMEM((2, half, depth), BF16),
            pltpu.VMEM((cells // LANES, LANES), F32),
            pltpu.VMEM((slots // LANES, LANES), BF16),
            pltpu.VMEM((slots, LANES), F32),
            pltpu.VMEM((2, half, cols), BF16),
            pltpu.VMEM((2, half, cols), BF16),
            pltpu.VMEM((2, half, cols), F32),
            pltpu.VMEM((2, half, cols), BF16),
            pltpu.VMEM((2, half, cols), BF16),
            pltpu.VMEM((2, 2, half, cols), BF16),
            pltpu.VMEM((pieces, 2 * share, width), BF16),
            pltpu.VMEM((pieces, 2 * share, width), BF16),
            pltpu.VMEM((pieces, 2 * share, width), F32),
            pltpu.VMEM((pieces, share, width), BF16),
            pltpu.VMEM((pieces, share, width), BF16),
            pltpu.VMEM((8, LANES), F32),
            pltpu.VMEM((group, 8, LANES), F32),
            pltpu.VMEM((8, LANES), F32),
            pltpu.VMEM((lines, 8, LANES), F32),
            pltpu.VMEM((mode_count // LANES, 1, LANES), F32),
            pltpu.VMEM((2, share, LANES), F32),
            dma((parts + 4 + pieces,)),
            dma((lines, group - 1 + lines - 1, parts)),
            dma((n, parts)),
            dma((4, 2)),
            dma((2,)),
            dma((2, pieces)),
            dma((2, pieces)),
            dma((group - 1 + lines - 1,)),
            dma((group,)),
            dma((lines,)),
        ],
        compiler_params=pltpu.CompilerParams(
            collective_id=0, has_side_effects=True, vmem_limit_bytes=58 * 1024 * 1024
        ),
    )(
        temporal_modes.astype(moved),
        volume_field,
        mass_root.reshape(cells // LANES, LANES),
        wall_pressure,
        face_area.reshape(slots // LANES, LANES),
        face_count,
    )
    return pl.pallas_call(
        deliver,
        out_shape=shapes,
        in_specs=[vmem, vmem],
        out_specs=(anywhere, anywhere),
        scratch_shapes=[dma((2,))],
        compiler_params=pltpu.CompilerParams(vmem_limit_bytes=1024 * 1024),
    )(*results)


def solution(mesh):
    in_specs = (
        P("cells", "snap"),
        P("snap", "cells"),
        P("cells"),
        P("cells", "snap"),
        P("cells"),
        P("cells"),
    )
    out_specs = (P("snap", "cells"), P("cells", None))
    return jax.shard_map(
        functools.partial(body, mesh.shape["cells"]),
        mesh=mesh, in_specs=in_specs, out_specs=out_specs, check_vma=False,
    )
```
